1024 devices in a mesh: replica: 16 (over z_lo), shard: 64 (over z_hi, y, x, core).
Axes of the slice: x: 4, y: 4, z: 32 (z_hi: 2, z_lo: 16; z = z_hi * 16 + z_lo), core: 2. Of those that a mesh axis runs over, the one named last changes fastest.
Arguments:
- pooled_grad: float32 [131072, 128], P(('replica', 'shard')), may hold values from -1.5 to 1.5
- bag_lengths: int32 [1024, 128], P(('replica', 'shard')), may hold values from 1 to 16, 1024 in all within a row
- slot_ids: int32 [1048576], P(('replica', 'shard')), may hold values from 0 to 511, as said below
- offsets: int32 [1048576], P(('replica', 'shard')), may hold values from 0 to 127
- touched_blocks: int32 [512], P('shard'), may hold values from 0 to 23, as said below
- embedding_table: float32 [196608, 128], P('shard'), may hold values from -3 to 3
- accumulator: float32 [196608], P('shard'), may hold values from 0.1 to 2
Outputs:
- new_table: float32 [196608, 128], P('shard')
- new_accumulator: float32 [196608], P('shard')
The draws below stay inside these ranges and needn't reach their ends.
Inputs may be any that keep to these rules, and one draw needn't show every extreme that they name: `slot_ids`: of the 1024 lookups of one device, exactly 32 name slots of one index o of shard (slots o * 8 to (o + 1) * 8 - 1), and every other index is named by at most 32 of them. `touched_blocks`: the 8 entries of one index of shard are distinct.
All inputs are finite; a program needn't handle non-finite values.
Results may differ from the reference program's by a relative error of at most 0.0003.
Values sent between devices are 32-bit elements; how exact they have to be, the bound alone decides.
A program may use at most 32 MiB of HBM per device.

```python
import math
import jax
import jax.numpy as jnp
import numpy as np
from jax import lax

D = 128
ROW_BLOCK = 128
S_DEV = 128
BLK_DEV = 24
TB = 8
BAG_MAX = 16
LK_DEV = 1024
CAP = 32
SAMPLES = 131072
LOOKUPS = 1048576
ROWS = 196608
N_SHARD = 64
DEVICES = 1024


def draw_slot_ids(key, part):
    key = jax.random.fold_in(key, 7)
    key_hot, key_shift, key_pick, key_order = jax.random.split(key, 4)
    hot_owner = jax.random.randint(key_hot, (DEVICES, 1), 0, N_SHARD)
    shift_by = jax.random.randint(key_shift, (DEVICES, 1), 0, N_SHARD - 1)
    position = jnp.arange(LK_DEV, dtype=jnp.int32)[None, :]
    spread = (hot_owner + 1 + (position - CAP + shift_by) % (N_SHARD - 1)) % N_SHARD
    owners = jnp.where(position < CAP, hot_owner, spread)
    order_keys = jax.random.split(key_order, DEVICES)
    orders = jax.vmap(lambda order_key: jax.random.permutation(order_key, LK_DEV))(order_keys)
    owners = jnp.take_along_axis(owners, orders, axis=1)
    picked = jax.random.randint(key_pick, (DEVICES, LK_DEV), 0, TB)
    return (owners * TB + picked).reshape(-1).astype(jnp.int32)


def draw_touched_blocks(key, part):
    key = jax.random.fold_in(key, 13)
    owner_keys = jax.random.split(key, N_SHARD)
    chosen = jax.vmap(lambda owner_key: jax.random.permutation(owner_key, BLK_DEV)[:TB])(owner_keys)
    return chosen.reshape(-1).astype(jnp.int32)


def with_ends(result, stream_key, smallest, largest):
    extent = result.shape
    index_at = [jax.random.randint(jax.random.fold_in(stream_key, axis), (), 0, extent[axis]) for axis in range(len(extent))]
    result = result.at[tuple(index_at)].set(smallest)
    longest = extent.index(max(extent))
    index_at[longest] = (index_at[longest] + 1) % extent[longest]
    return result.at[tuple(index_at)].set(largest)


def block_scale(stream_key, shape, cuts, low, largest):
    level, own = 1.0, jax.random.fold_in(stream_key, 6)
    for axis_at, shards_of in cuts:
        steps = jnp.exp(jax.random.uniform(jax.random.fold_in(own, axis_at), (shards_of,), jnp.float32, low / len(cuts), largest / len(cuts)))
        level = level * jnp.repeat(steps, shape[axis_at] // shards_of).reshape([-1 if axis == axis_at else 1 for axis in range(len(shape))])
    return level


def split_up(count, total, bound, lean):
    portions = [(1 << 20) // math.isqrt(standing ** lean) + 1 for standing in range(2, count + 1)]
    rest, holding = total - bound - (count - 1), [1] * (count - 1)
    while rest > 0:
        free = [i for i in range(count - 1) if holding[i] < bound]
        whole, left = sum([portions[i] for i in free]), rest
        for i in free:
            addition = min(bound - holding[i], max(1, left * portions[i] // whole), rest)
            holding[i] = holding[i] + addition
            rest = rest - addition
    return np.array([bound] + holding)


def uneven_parts(rng, amount, total, bound, lean):
    if amount == 2:
        one = jax.random.randint(rng, (), max(1, total - bound), min(bound, total - 1) + 1)
        return jnp.stack([one, total - one])
    tallies = jnp.asarray(split_up(amount, total, bound, lean), jnp.int32)
    twos = (amount - 1) // 2
    giver, sink = tallies[1:1 + 2 * twos:2], tallies[2:2 + 2 * twos:2]
    margin = jnp.minimum(giver - 1, bound - sink)
    passed = jax.random.randint(jax.random.fold_in(rng, 1), (twos,), 0, 1 << 20) % (margin + 1)
    tallies = tallies.at[1:1 + 2 * twos:2].set(giver - passed).at[2:2 + 2 * twos:2].set(sink + passed)
    return tallies[jax.random.permutation(jax.random.fold_in(rng, 2), amount)]


def centred(rng, extent, scale, reach, shards=(), kind=jnp.bfloat16):
    result = jax.random.normal(rng, extent, jnp.float32) * scale
    if len(shards) > 0:
        result = block_scale(rng, extent, shards, -0.22, 0.18) * result
    return jnp.clip(result, min=-reach, max=reach).astype(kind)


def setup_inputs(seed: int = 0) -> dict:
    streams_of = jax.random.split(jax.random.key(seed), 8)
    return {
        "pooled_grad": centred(streams_of[0], (SAMPLES, D), 0.25, 1.5, ((0, 1024),), jnp.float32),
        "bag_lengths": jax.vmap(lambda own: uneven_parts(own, S_DEV, LK_DEV, BAG_MAX, 2))(jax.random.split(streams_of[1], DEVICES)).reshape((DEVICES, S_DEV)).astype(jnp.int32),
        "slot_ids": draw_slot_ids(jax.random.fold_in(streams_of[7], 71), 0),
        "offsets": with_ends(jax.random.randint(streams_of[3], (LOOKUPS,), 0, ROW_BLOCK), jax.random.fold_in(streams_of[3], 1), 0, ROW_BLOCK - 1).astype(jnp.int32),
        "touched_blocks": draw_touched_blocks(jax.random.fold_in(streams_of[7], 71), 0),
        "embedding_table": centred(streams_of[5], (ROWS, D), 0.5, 3.0, ((0, 64),), jnp.float32),
        "accumulator": jnp.clip(jnp.exp(math.log(2.0) - 2.9957323 * jax.random.uniform(streams_of[6], (ROWS,), jnp.float32) ** block_scale(streams_of[6], (ROWS,), ((0, 64),), -0.2, 0.2)), 0.1, 2.0),
    }


learning_rate = 0.5
epsilon = 1e-08

def reference(pooled_grad, bag_lengths, slot_ids, offsets, touched_blocks, embedding_table, accumulator):
    bag_ends = jnp.cumsum(bag_lengths, axis=1).astype(jnp.int32)
    positions = jnp.arange(LK_DEV, dtype=jnp.int32)
    local_sample = jax.vmap(lambda bag_end: jnp.searchsorted(bag_end, positions, side='right'))(bag_ends).astype(jnp.int32)
    sample_of = local_sample + (jnp.arange(DEVICES, dtype=jnp.int32) * S_DEV)[:, None]
    owner_index = (slot_ids // TB).astype(jnp.int32)
    global_block = owner_index * BLK_DEV + touched_blocks[slot_ids]
    row_of = (global_block * ROW_BLOCK + offsets).astype(jnp.int32).reshape(DEVICES, LK_DEV)

    def add_device(gradient, pieces):
        device_rows, device_samples = pieces
        return (gradient.at[device_rows].add(pooled_grad[device_samples].astype(jnp.float32)), None)
    gradient, _ = lax.scan(add_device, jnp.zeros((ROWS, D), jnp.float32), (row_of, sample_of))
    new_accumulator = accumulator + lax.optimization_barrier(jnp.mean(gradient * gradient, axis=1))
    new_table = embedding_table - learning_rate * gradient / (jnp.sqrt(new_accumulator) + epsilon)[:, None]
    return (new_table, new_accumulator)
```

```python
import jax
import jax.numpy as jnp
from jax import lax
from jax.experimental import pallas as pl
from jax.experimental.pallas import tpu as pltpu
from jax.sharding import PartitionSpec as P

MESH = pl.DeviceIdType.MESH
F32, BF16, I32 = jnp.float32, jnp.bfloat16, jnp.int32

learning_rate = 0.5
epsilon = 1e-08

GROUP = 64
CAP = 32
BLOCKS = 8
ROWS = 128
D = 128
LOOKUPS = 1024


def dot(a, b):
    return lax.dot_general(a, b, (((1,), (0,)), ((), ())), preferred_element_type=F32)


def dot_t(a, b):
    return lax.dot_general(a, b, (((1,), (1,)), ((), ())), preferred_element_type=F32)


def iota(shape, dim):
    return lax.broadcasted_iota(I32, shape, dim)


def halves(x):
    high = x.astype(BF16)
    return high, (x - high.astype(F32)).astype(BF16)


def rows_side_by_side(parts):
    return jnp.concatenate(parts, axis=1)


def gather_kernel(
    grad_ref, len_ref, slot_ref, off_ref, total_ref,
    sbuf, rbuf, sid, rid, rhl, looked, partial, left_in, right_in,
    send_sem, recv_sem, sid_sem, rid_sem, red_send, left_sem, right_sem, out_send, out_sem,
):
    replica, shard = lax.axis_index("replica"), lax.axis_index("shard")
    z = lax.div(shard, 32) * 16 + replica
    within = lax.rem(shard, 32)
    parity = lax.rem(z, 2)
    me = parity * 32 + within

    def device(z_at, place):
        return (lax.rem(z_at, 16), lax.div(z_at, 16) * 32 + place)

    def member(o):
        return device(z - parity + lax.div(o, 32), lax.rem(o, 32))

    left = device(lax.rem(z + 30, 32), within)
    right = device(lax.rem(z + 2, 32), within)
    twin = device(z + 1 - 2 * parity, within)

    barrier = pltpu.get_barrier_semaphore()

    def greet(i, carry):
        pl.semaphore_signal(
            barrier, inc=1, device_id=member(lax.rem(me + i, GROUP)), device_id_type=MESH
        )
        return carry

    lax.fori_loop(1, GROUP, greet, 0)
    for other in (left, right):
        pl.semaphore_signal(barrier, inc=1, device_id=other, device_id_type=MESH)

    row, col = iota((128, 128), 0), iota((128, 128), 1)
    upto = (row <= col).astype(F32).astype(BF16)
    before = (row < col).astype(F32).astype(BF16)
    lengths = len_ref[...].astype(F32)
    ends = dot(jnp.broadcast_to(lengths, (8, 128)).astype(BF16), upto)[0:1, :]
    starts = ends - lengths
    position = iota((LOOKUPS, 128), 0).astype(F32)
    sample_hot = jnp.where((position >= starts) & (position < ends), 1.0, 0.0).astype(BF16)
    high, low = halves(grad_ref[...])
    looked[...] = dot(sample_hot, jnp.concatenate([high, low], axis=1)).astype(BF16)

    slots = slot_ref[...]
    owner = lax.shift_right_logical(slots, 3)
    listed = slots - owner * BLOCKS
    owner_hot = [
        jnp.where(owner[b : b + 1, :] == iota((GROUP, 128), 0), 1.0, 0.0) for b in range(8)
    ]
    counts = dot(jnp.concatenate(owner_hot, axis=0).astype(BF16), before)
    seen = jnp.zeros((GROUP, 1), F32)
    ranks = []
    for b in range(8):
        earlier = counts[b * GROUP : (b + 1) * GROUP, :] + seen
        ranks.append(jnp.sum(owner_hot[b] * earlier, axis=0, keepdims=True))
        seen = seen + jnp.sum(owner_hot[b], axis=1, keepdims=True)
    rank = rows_side_by_side(ranks)
    owner_row = rows_side_by_side([owner[b : b + 1, :] for b in range(8)])
    place = owner_row * CAP + rank.astype(I32)
    owners = rows_side_by_side([h.astype(BF16) for h in owner_hot])
    lane = rank.astype(I32) + CAP * lax.rem(me, 4)
    at_lane = lane == iota((128, LOOKUPS), 0)
    listed_row = rows_side_by_side([listed[b : b + 1, :] for b in range(8)]).astype(F32)
    offset_row = rows_side_by_side([off_ref[b : b + 1, :] for b in range(8)]).astype(F32)
    ids = 128.0 * dot_t(owners, jnp.where(at_lane, listed_row + 1.0, 0.0).astype(BF16)) + dot_t(
        owners, jnp.where(at_lane, offset_row, 0.0).astype(BF16)
    )
    for o in range(GROUP):
        sid[o] = ids[o : o + 1, :]

    pl.semaphore_wait(barrier, GROUP + 1)

    def value_copy(o, src):
        return pltpu.make_async_remote_copy(
            sbuf.at[o], rbuf.at[src], send_sem.at[o], recv_sem.at[src],
            device_id=member(o), device_id_type=MESH,
        )

    def id_copy(o, src):
        return pltpu.make_async_remote_copy(
            sid.at[o], rid.at[src], sid_sem.at[o], rid_sem.at[src],
            device_id=member(o), device_id_type=MESH,
        )

    my_quad = lax.div(me, 4)

    def send(i, carry):
        quad = lax.rem(my_quad + 1 + i, 16)
        hot = jnp.where(place - quad * 128 == iota((128, LOOKUPS), 0), 1.0, 0.0).astype(BF16)
        both = dot(hot, looked[...])
        sbuf[pl.ds(quad * 4, 4)] = (both[:, :D] + both[:, D:]).reshape(4, CAP, D)
        for r in range(4):
            o = quad * 4 + r

            @pl.when(o != me)
            def _():
                value_copy(o, me).start()
                id_copy(o, me).start()

        return carry

    lax.fori_loop(0, 16, send, 0)
    rbuf[me] = sbuf[me]
    rid[me] = sid[me]

    def arrive(i, carry):
        src = lax.rem(me + i, GROUP)
        value_copy(src, src).wait_recv()
        id_copy(src, src).wait_recv()
        return carry

    lax.fori_loop(1, GROUP, arrive, 0)

    id_row = rows_side_by_side(
        [rid[4 * g] + rid[4 * g + 1] + rid[4 * g + 2] + rid[4 * g + 3] for g in range(16)]
    ).astype(I32)
    high, low = halves(rbuf[...].reshape(GROUP * CAP, D))
    rhl[:, :D] = high
    rhl[:, D:] = low

    def own_block(j):
        hot = jnp.where(
            id_row - (j + 1) * ROWS == iota((ROWS, GROUP * CAP), 0), 1.0, 0.0
        ).astype(BF16)
        both = dot(hot, rhl[...])
        return both[:, :D] + both[:, D:]

    seat = lax.rem(lax.div(z, 2) - 8 * parity + 16, 16)

    def left_copy(j):
        return pltpu.make_async_remote_copy(
            partial.at[j], left_in.at[j], red_send.at[j], left_sem.at[j],
            device_id=left, device_id_type=MESH,
        )

    def right_copy(j):
        return pltpu.make_async_remote_copy(
            partial.at[j], right_in.at[j], red_send.at[j], right_sem.at[j],
            device_id=right, device_id_type=MESH,
        )

    def reduce_step(t, carry):
        jl = lax.rem(seat + 8 + t, 16)
        jr = lax.rem(seat + 23 - t, 16)

        @pl.when(jl < BLOCKS)
        def _():
            partial[jl] = own_block(jl)

        @pl.when((jr < BLOCKS) & (t < 7))
        def _():
            partial[jr] = own_block(jr)

        @pl.when(jl < BLOCKS)
        def _():
            @pl.when(t > 0)
            def _():
                left_copy(jl).wait_recv()
                partial[jl] = partial[jl] + left_in[jl]

            left_copy(jl).start()

        @pl.when((jr < BLOCKS) & (t < 7))
        def _():
            @pl.when(t > 0)
            def _():
                right_copy(jr).wait_recv()
                partial[jr] = partial[jr] + right_in[jr]

            right_copy(jr).start()

        return carry

    lax.fori_loop(0, 8, reduce_step, 0)

    def out_copy(j, way, target):
        return pltpu.make_async_remote_copy(
            total_ref.at[j], total_ref.at[j], out_send.at[j, way], out_sem.at[j],
            device_id=target, device_id_type=MESH,
        )

    holds = seat < BLOCKS

    @pl.when(holds)
    def _():
        mine = own_block(seat)
        left_copy(seat).wait_recv()
        right_copy(seat).wait_recv()
        total_ref[seat] = mine + left_in[seat] + right_in[seat]

        @pl.when(seat > 0)
        def _():
            out_copy(seat, 0, left).start()

        @pl.when(seat < 7)
        def _():
            out_copy(seat, 1, right).start()

        out_copy(seat, 2, twin).start()

        def pass_on(s, carry):
            @pl.when(seat + s < BLOCKS)
            def _():
                out_copy(seat + s, 0, left).wait_recv()

                @pl.when(seat > 0)
                def _():
                    out_copy(seat + s, 0, left).start()

                out_copy(seat + s, 2, twin).start()

            @pl.when(seat - s >= 0)
            def _():
                out_copy(seat - s, 1, right).wait_recv()

                @pl.when(seat < 7)
                def _():
                    out_copy(seat - s, 1, right).start()

                out_copy(seat - s, 2, twin).start()

            return carry

        lax.fori_loop(1, 8, pass_on, 0)

        def sent(j, carry):
            @pl.when((j >= seat) & (seat > 0))
            def _():
                out_copy(j, 0, left).wait_send()

            @pl.when((j <= seat) & (seat < 7))
            def _():
                out_copy(j, 1, right).wait_send()

            out_copy(j, 2, twin).wait_send()
            return carry

        lax.fori_loop(0, BLOCKS, sent, 0)

    @pl.when(jnp.logical_not(holds))
    def _():
        def land(j, carry):
            out_copy(j, 2, twin).wait_recv()
            return carry

        lax.fori_loop(0, BLOCKS, land, 0)

    def reduced(j, carry):
        @pl.when(j != seat)
        def _():
            left_copy(j).wait_send()

        return carry

    lax.fori_loop(0, BLOCKS, reduced, 0)

    def gone(i, carry):
        o = lax.rem(me + i, GROUP)
        value_copy(o, me).wait_send()
        id_copy(o, me).wait_send()
        return carry

    lax.fori_loop(1, GROUP, gone, 0)


def update_kernel(touched_ref, total_ref, table_ref, accum_ref, table_out, accum_out, at_block):
    table_out[...] = table_ref[...]
    accum_out[...] = accum_ref[...]
    at_block[...] = jnp.zeros_like(at_block)
    for j in range(BLOCKS):
        at_block[j : j + 1, :] = accum_ref[pl.ds(touched_ref[j], 1), :]
    old = at_block[...].T
    new = old
    lanes = iota((ROWS, ROWS), 1)
    for j in range(BLOCKS):
        gradient = total_ref[j]
        rows = old[:, j : j + 1] + jnp.sum(gradient * gradient, axis=1, keepdims=True) * (1.0 / D)
        new = jnp.where(lanes == j, rows, new)
        first = pl.multiple_of(touched_ref[j] * ROWS, ROWS)
        table_out[pl.ds(first, ROWS), :] = table_ref[pl.ds(first, ROWS), :] - (
            learning_rate * gradient / (jnp.sqrt(rows) + epsilon)
        )
    at_block[...] = new.T
    for j in range(BLOCKS):
        accum_out[pl.ds(touched_ref[j], 1), :] = at_block[j : j + 1, :]


def on_device(
    pooled_grad, bag_lengths, slot_ids, offsets, touched_blocks, embedding_table, accumulator
):
    vmem = pl.BlockSpec(memory_space=pltpu.VMEM)
    smem = pl.BlockSpec(memory_space=pltpu.SMEM)
    dma = pltpu.SemaphoreType.DMA
    total = pl.pallas_call(
        gather_kernel,
        out_shape=jax.ShapeDtypeStruct((BLOCKS, ROWS, D), F32),
        in_specs=[vmem] * 4,
        out_specs=vmem,
        scratch_shapes=[
            pltpu.VMEM((GROUP, CAP, D), F32),
            pltpu.VMEM((GROUP, CAP, D), F32),
            pltpu.VMEM((GROUP, 1, 128), F32),
            pltpu.VMEM((GROUP, 1, 128), F32),
            pltpu.VMEM((GROUP * CAP, 2 * D), BF16),
            pltpu.VMEM((LOOKUPS, 2 * D), BF16),
            pltpu.VMEM((BLOCKS, ROWS, D), F32),
            pltpu.VMEM((BLOCKS, ROWS, D), F32),
            pltpu.VMEM((BLOCKS, ROWS, D), F32),
            dma((GROUP,)), dma((GROUP,)), dma((GROUP,)), dma((GROUP,)),
            dma((BLOCKS,)), dma((BLOCKS,)), dma((BLOCKS,)),
            dma((BLOCKS, 3)), dma((BLOCKS,)),
        ],
        compiler_params=pltpu.CompilerParams(
            collective_id=0, has_side_effects=True, vmem_limit_bytes=40 << 20
        ),
        name="exchange",
    )(pooled_grad, bag_lengths, slot_ids.reshape(8, 128), offsets.reshape(8, 128))
    rows = embedding_table.shape[0]
    new_table, new_accumulator = pl.pallas_call(
        update_kernel,
        out_shape=(
            jax.ShapeDtypeStruct((rows, D), F32),
            jax.ShapeDtypeStruct((rows // ROWS, ROWS), F32),
        ),
        in_specs=[smem, vmem, vmem, vmem],
        out_specs=(vmem, vmem),
        scratch_shapes=[pltpu.VMEM((ROWS, ROWS), F32)],
        compiler_params=pltpu.CompilerParams(vmem_limit_bytes=40 << 20),
        name="adagrad",
    )(touched_blocks, total, embedding_table, accumulator.reshape(rows // ROWS, ROWS))
    return new_table, new_accumulator.reshape(rows)


def solution(mesh):
    return jax.shard_map(
        on_device,
        mesh=mesh,
        in_specs=(
            P(("replica", "shard"), None),
            P(("replica", "shard"), None),
            P(("replica", "shard")),
            P(("replica", "shard")),
            P("shard"),
            P("shard", None),
            P("shard"),
        ),
        out_specs=(P("shard", None), P("shard")),
        check_vma=False,
    )
```

```python
import jax
import jax.numpy as jnp
from jax import lax
from jax.experimental import pallas as pl
from jax.experimental.pallas import tpu as pltpu
from jax.sharding import PartitionSpec as P

MESH = pl.DeviceIdType.MESH
F32, BF16, I32 = jnp.float32, jnp.bfloat16, jnp.int32

learning_rate = 0.5
epsilon = 1e-08

GROUP = 64
CAP = 32
BLOCKS = 8
ROWS = 128
D = 128
LOOKUPS = 1024
PIECES, PIECE = 16, 64
HOLDERS = 4


def dot(a, b):
    return lax.dot_general(a, b, (((1,), (0,)), ((), ())), preferred_element_type=F32)


def dot_t(a, b):
    return lax.dot_general(a, b, (((1,), (1,)), ((), ())), preferred_element_type=F32)


def iota(shape, dim):
    return lax.broadcasted_iota(I32, shape, dim)


def halves(x):
    high = x.astype(BF16)
    return high, (x - high.astype(F32)).astype(BF16)


def rows_side_by_side(parts):
    return jnp.concatenate(parts, axis=1)


def gather_kernel(
    grad_hbm, len_hbm, slot_hbm, off_hbm, total_ref,
    grad_ref, len_ref, slot_ref, off_ref, sbuf, rbuf, rhl, looked, partial,
    left_in, left_side, right_in, right_side,
    copy_sem, send_sem, recv_sem, red_send,
    left_sem, left_side_sem, right_sem, right_side_sem, out_send, out_sem,
):
    loads = [
        pltpu.make_async_copy(src, dst, copy_sem.at[i])
        for i, (src, dst) in enumerate(
            ((grad_hbm, grad_ref), (len_hbm, len_ref), (slot_hbm, slot_ref), (off_hbm, off_ref))
        )
    ]
    for load in loads:
        load.start()

    replica, shard = lax.axis_index("replica"), lax.axis_index("shard")
    z = lax.div(shard, 32) * 16 + replica
    within = lax.rem(shard, 32)
    parity = lax.rem(z, 2)
    sign = 1 - 2 * parity

    def number(plane, y_at, rest):
        return plane * 32 + lax.rem(y_at - lax.div(rest, 2) + 4, 4) * 8 + rest

    me = number(parity, lax.div(within, 8), lax.rem(within, 8))

    def device(z_at, place):
        return (lax.rem(z_at, 16), lax.div(z_at, 16) * 32 + place)

    def member(o):
        rest = lax.rem(o, 8)
        y_at = lax.rem(lax.div(o, 8) + lax.div(rest, 2), 4)
        return device(z - parity + lax.div(o, 32), y_at * 8 + rest)

    seat = parity * lax.div(31 - z, 2) + (1 - parity) * lax.div(z, 2)

    def along(steps):
        return device(lax.rem(z + sign * steps + 32, 32), within)

    left, right, far_left, far_right = along(-2), along(2), along(-4), along(4)
    twin, inner = along(1), along(-1)

    barrier = pltpu.get_barrier_semaphore()

    def greet(i, carry):
        pl.semaphore_signal(
            barrier, inc=1, device_id=member(lax.rem(me + i, GROUP)), device_id_type=MESH
        )
        return carry

    for other in (left, right, far_left, far_right, inner):
        pl.semaphore_signal(barrier, inc=1, device_id=other, device_id_type=MESH)
    lax.fori_loop(1, GROUP, greet, 0)
    for load in loads:
        load.wait()

    row, col = iota((128, 128), 0), iota((128, 128), 1)
    upto = (row <= col).astype(F32).astype(BF16)
    before = (row < col).astype(F32).astype(BF16)
    lengths = len_ref[...].astype(F32)
    ends = dot(jnp.broadcast_to(lengths, (8, 128)).astype(BF16), upto)[0:1, :]
    starts = ends - lengths
    position = iota((LOOKUPS, 128), 0).astype(F32)
    sample_hot = jnp.where((position >= starts) & (position < ends), 1.0, 0.0).astype(BF16)
    high, low = halves(grad_ref[...])
    looked[...] = dot(sample_hot, jnp.concatenate([high, low], axis=1)).astype(BF16)

    slots = slot_ref[...]
    listed = lax.rem(slots, BLOCKS)
    index = lax.div(slots, BLOCKS)
    owner = number(lax.div(index, 32), lax.rem(lax.div(index, 8), 4), lax.rem(index, 8))
    owner_hot = [
        jnp.where(owner[b : b + 1, :] == iota((GROUP, 128), 0), 1.0, 0.0) for b in range(8)
    ]
    counts = dot(jnp.concatenate(owner_hot, axis=0).astype(BF16), before)
    seen = jnp.zeros((GROUP, 1), F32)
    ranks = []
    for b in range(8):
        earlier = counts[b * GROUP : (b + 1) * GROUP, :] + seen
        ranks.append(jnp.sum(owner_hot[b] * earlier, axis=0, keepdims=True))
        seen = seen + jnp.sum(owner_hot[b], axis=1, keepdims=True)
    rank = rows_side_by_side(ranks)
    owner_row = rows_side_by_side([owner[b : b + 1, :] for b in range(8)])
    place = owner_row * CAP + rank.astype(I32)
    owners = rows_side_by_side([h.astype(BF16) for h in owner_hot])
    lane = rank.astype(I32) + CAP * lax.rem(me, 4)
    at_lane = lane == iota((128, LOOKUPS), 0)
    listed_row = rows_side_by_side([listed[b : b + 1, :] for b in range(8)]).astype(F32)
    offset_row = rows_side_by_side([off_ref[b : b + 1, :] for b in range(8)]).astype(F32)
    ids = 128.0 * dot_t(owners, jnp.where(at_lane, listed_row + 1.0, 0.0).astype(BF16)) + dot_t(
        owners, jnp.where(at_lane, offset_row, 0.0).astype(BF16)
    )
    for o in range(GROUP):
        sbuf[o, CAP : CAP + 1, :] = ids[o : o + 1, :]

    pl.semaphore_wait(barrier, GROUP + 4)

    def value_copy(o, src):
        return pltpu.make_async_remote_copy(
            sbuf.at[o, pl.ds(0, CAP + 1)], rbuf.at[src, pl.ds(0, CAP + 1)], send_sem.at[o], recv_sem.at[src],
            device_id=member(o), device_id_type=MESH,
        )

    my_oct = lax.div(me, 8)

    def send(i, carry):
        oct_at = lax.rem(my_oct + 1 + i, 8)
        hot = jnp.where(place - oct_at * 256 == iota((256, LOOKUPS), 0), 1.0, 0.0).astype(BF16)
        both = dot(hot, looked[...])
        sbuf[pl.ds(oct_at * 8, 8), pl.ds(0, CAP), :] = (both[:, :D] + both[:, D:]).reshape(8, CAP, D)
        for r in range(8):
            o = oct_at * 8 + lax.rem(me + r, 8)

            @pl.when(o != me)
            def _():
                value_copy(o, me).start()

        return carry

    lax.fori_loop(0, 8, send, 0)
    rbuf[me, pl.ds(0, CAP), :] = sbuf[me, pl.ds(0, CAP), :]
    rbuf[me, pl.ds(CAP, 1), :] = sbuf[me, pl.ds(CAP, 1), :]

    def arrive(i, carry):
        src = lax.rem(me + i, GROUP)
        value_copy(src, src).wait_recv()
        return carry

    lax.fori_loop(1, GROUP, arrive, 0)

    id_row = rows_side_by_side(
        [sum(rbuf[4 * g + r, CAP : CAP + 1, :] for r in range(4)) for g in range(16)]
    ).astype(I32)
    high, low = halves(rbuf[:, :CAP, :].reshape(GROUP * CAP, D))
    rhl[:, :D] = high
    rhl[:, D:] = low

    def own_pieces(h):
        hot = jnp.where(
            id_row - (h * 256 + 128) == iota((256, GROUP * CAP), 0), 1.0, 0.0
        ).astype(BF16)
        both = dot(hot, rhl[...])
        partial[pl.ds(h * 4, 4)] = (both[:, :D] + both[:, D:]).reshape(4, PIECE, D)

    def hop(q, into, sem, target):
        return pltpu.make_async_remote_copy(
            partial.at[q], into.at[q], red_send.at[q], sem.at[q],
            device_id=target, device_id_type=MESH,
        )

    def side_step(h, into, sem, target):
        @pl.when(h < HOLDERS)
        def _():
            own_pieces(h)

            def one(k, carry):
                hop(h * 4 + k, into, sem, target).start()
                return carry

            lax.fori_loop(0, 4, one, 0)

    def place_of(steps):
        return lax.rem(seat - 2 + steps + 32, 16)

    def reduce_step(t, carry):
        ahead = 8 - 2 * t
        h_left, h_right = place_of(-ahead), place_of(ahead)
        leads_left, leads_right = h_left < HOLDERS, (h_right < HOLDERS) & (t > 0)

        @pl.when(leads_left & (t == 0))
        def _():
            own_pieces(h_left)

            def one(k, carry):
                hop(h_left * 4 + k, left_in, left_sem, far_left).start()
                return carry

            lax.fori_loop(0, 4, one, 0)

        side_step(place_of(1 - ahead), left_side, left_side_sem, left)
        side_step(place_of(ahead - 1), right_side, right_side_sem, right)

        @pl.when(leads_left & (t > 0))
        def _():
            own_pieces(h_left)

        @pl.when(leads_right)
        def _():
            own_pieces(h_right)

        def one(k, carry):
            @pl.when(leads_left & (t > 0))
            def _():
                q = h_left * 4 + k
                hop(q, left_side, left_side_sem, left).wait_recv()
                hop(q, left_in, left_sem, far_left).wait_recv()
                partial[q] = partial[q] + left_side[q] + left_in[q]
                hop(q, left_in, left_sem, far_left).start()

            @pl.when(leads_right)
            def _():
                q = h_right * 4 + k
                hop(q, right_side, right_side_sem, right).wait_recv()

                @pl.when(t > 1)
                def _():
                    hop(q, right_in, right_sem, far_right).wait_recv()
                    partial[q] = partial[q] + right_in[q]

                partial[q] = partial[q] + right_side[q]
                hop(q, right_in, right_sem, far_right).start()

            return carry

        lax.fori_loop(0, 4, one, 0)
        return carry

    lax.fori_loop(0, 4, reduce_step, 0)

    def out_copy(q, way, target):
        return pltpu.make_async_remote_copy(
            total_ref.at[q], total_ref.at[q], out_send.at[q, way], out_sem.at[q],
            device_id=target, device_id_type=MESH,
        )

    main = seat < 8
    mine = seat - 2
    holds = (seat >= 2) & (seat < 2 + HOLDERS)

    @pl.when(holds)
    def _():
        own_pieces(mine)

        def one(k, carry):
            q = mine * 4 + k
            hop(q, left_side, left_side_sem, left).wait_recv()
            hop(q, right_side, right_side_sem, right).wait_recv()
            hop(q, right_in, right_sem, far_right).wait_recv()
            hop(q, left_in, left_sem, far_left).wait_recv()
            total_ref[q] = (
                partial[q] + left_side[q] + right_side[q] + left_in[q] + right_in[q]
            )
            out_copy(q, 0, left).start()
            out_copy(q, 1, right).start()
            return carry

        lax.fori_loop(0, 4, one, 0)

    @pl.when(main)
    def _():
        def pass_on(s, carry):
            def one(k, carry):
                @pl.when((mine + s >= 0) & (mine + s < HOLDERS))
                def _():
                    q = (mine + s) * 4 + k
                    out_copy(q, 0, left).wait_recv()

                    @pl.when(seat > 0)
                    def _():
                        out_copy(q, 0, left).start()

                    out_copy(q, 2, twin).start()

                @pl.when((mine - s >= 0) & (mine - s < HOLDERS))
                def _():
                    q = (mine - s) * 4 + k
                    out_copy(q, 1, right).wait_recv()

                    @pl.when(seat < 7)
                    def _():
                        out_copy(q, 1, right).start()

                    out_copy(q, 2, inner).start()

                    @pl.when(seat == 7)
                    def _():
                        out_copy(q, 3, twin).start()

                return carry

            return lax.fori_loop(0, 4, one, carry)

        lax.fori_loop(1, 6, pass_on, 0)

        def sent(q, carry):
            h = lax.div(q, 4)

            @pl.when((h >= mine) & (seat > 0))
            def _():
                out_copy(q, 0, left).wait_send()

            @pl.when((h <= mine) & (seat < 7))
            def _():
                out_copy(q, 1, right).wait_send()

            @pl.when(h != mine)
            def _():
                out_copy(q, 2, twin).wait_send()

            @pl.when(seat == 7)
            def _():
                out_copy(q, 3, twin).wait_send()

            return carry

        lax.fori_loop(0, PIECES, sent, 0)

    @pl.when(jnp.logical_not(main))
    def _():
        def land(q, carry):
            out_copy(q, 2, twin).wait_recv()
            return carry

        lax.fori_loop(0, PIECES, land, 0)

    def reduced(q, carry):
        @pl.when(lax.div(q, 4) != mine)
        def _():
            hop(q, left_in, left_sem, left).wait_send()

        return carry

    lax.fori_loop(0, PIECES, reduced, 0)

    def gone(i, carry):
        o = lax.rem(me + i, GROUP)
        value_copy(o, me).wait_send()
        return carry

    lax.fori_loop(1, GROUP, gone, 0)


def update_kernel(
    touched_hbm, total_hbm, table_hbm, accum_hbm, table_out, accum_out,
    total_ref, table_ref, accum_ref, at_block, touched_ref, sem,
):
    load_total = pltpu.make_async_copy(total_hbm, total_ref, sem.at[5])
    load_total.start()
    load_touched = pltpu.make_async_copy(touched_hbm, touched_ref, sem.at[4])
    load_touched.start()
    load_table = pltpu.make_async_copy(table_hbm, table_ref, sem.at[0])
    load_accum = pltpu.make_async_copy(accum_hbm, accum_ref, sem.at[1])
    load_accum.start()
    load_table.start()
    load_total.wait()
    squares = [
        jnp.sum(total_ref[j] * total_ref[j], axis=1, keepdims=True) * (1.0 / D)
        for j in range(BLOCKS)
    ]
    load_touched.wait()
    load_accum.wait()
    at_block[...] = jnp.zeros_like(at_block)
    for j in range(BLOCKS):
        at_block[j : j + 1, :] = accum_ref[pl.ds(touched_ref[j], 1), :]
    old = at_block[...].T
    new = old
    lanes = iota((ROWS, ROWS), 1)
    steps = []
    for j in range(BLOCKS):
        rows = old[:, j : j + 1] + squares[j]
        new = jnp.where(lanes == j, rows, new)
        steps.append(jnp.sqrt(rows) + epsilon)
    at_block[...] = new.T
    for j in range(BLOCKS):
        accum_ref[pl.ds(touched_ref[j], 1), :] = at_block[j : j + 1, :]
    save_accum = pltpu.make_async_copy(accum_ref, accum_out, sem.at[3])
    save_accum.start()
    load_table.wait()
    for j in range(BLOCKS):
        first = pl.multiple_of(touched_ref[j] * ROWS, ROWS)
        table_ref[pl.ds(first, ROWS), :] = table_ref[pl.ds(first, ROWS), :] - (
            learning_rate * total_ref[j] / steps[j]
        )
    save_table = pltpu.make_async_copy(table_ref, table_out, sem.at[2])
    save_table.start()
    save_accum.wait()
    save_table.wait()


def on_device(
    pooled_grad, bag_lengths, slot_ids, offsets, touched_blocks, embedding_table, accumulator
):
    vmem = pl.BlockSpec(memory_space=pltpu.VMEM)
    hbm = pl.BlockSpec(memory_space=pltpu.HBM)
    dma = pltpu.SemaphoreType.DMA
    pieces = pltpu.VMEM((PIECES, PIECE, D), F32)
    total = pl.pallas_call(
        gather_kernel,
        out_shape=jax.ShapeDtypeStruct((PIECES, PIECE, D), F32),
        in_specs=[hbm] * 4,
        out_specs=vmem,
        scratch_shapes=[
            pltpu.VMEM((128, D), F32),
            pltpu.VMEM((1, 128), I32),
            pltpu.VMEM((8, 128), I32),
            pltpu.VMEM((8, 128), I32),
            pltpu.VMEM((GROUP, CAP + 8, D), F32),
            pltpu.VMEM((GROUP, CAP + 8, D), F32),
            pltpu.VMEM((GROUP * CAP, 2 * D), BF16),
            pltpu.VMEM((LOOKUPS, 2 * D), BF16),
            pieces, pieces, pieces, pieces, pieces,
            dma((4,)),
            dma((GROUP,)), dma((GROUP,)),
            dma((PIECES,)), dma((PIECES,)), dma((PIECES,)), dma((PIECES,)), dma((PIECES,)),
            dma((PIECES, 4)), dma((PIECES,)),
        ],
        compiler_params=pltpu.CompilerParams(
            collective_id=0, has_side_effects=True, vmem_limit_bytes=63 << 20
        ),
        name="exchange",
    )(pooled_grad, bag_lengths, slot_ids.reshape(8, 128), offsets.reshape(8, 128))
    rows = embedding_table.shape[0]
    new_table, new_accumulator = pl.pallas_call(
        update_kernel,
        out_shape=(
            jax.ShapeDtypeStruct((rows, D), F32),
            jax.ShapeDtypeStruct((rows // ROWS, ROWS), F32),
        ),
        in_specs=[hbm, hbm, hbm, hbm],
        out_specs=(hbm, hbm),
        scratch_shapes=[
            pltpu.VMEM((BLOCKS, ROWS, D), F32),
            pltpu.VMEM((rows, D), F32),
            pltpu.VMEM((rows // ROWS, ROWS), F32),
            pltpu.VMEM((ROWS, ROWS), F32),
            pltpu.SMEM((BLOCKS,), I32),
            dma((6,)),
        ],
        compiler_params=pltpu.CompilerParams(vmem_limit_bytes=63 << 20),
        name="adagrad",
    )(
        touched_blocks, total.reshape(BLOCKS, ROWS, D), embedding_table,
        accumulator.reshape(rows // ROWS, ROWS),
    )
    return new_table, new_accumulator.reshape(rows)


def solution(mesh):
    return jax.shard_map(
        on_device,
        mesh=mesh,
        in_specs=(
            P(("replica", "shard"), None),
            P(("replica", "shard"), None),
            P(("replica", "shard")),
            P(("replica", "shard")),
            P("shard"),
            P("shard", None),
            P("shard"),
        ),
        out_specs=(P("shard", None), P("shard")),
        check_vma=False,
    )
```

```python
import jax
import jax.numpy as jnp
from jax import lax
from jax.experimental import pallas as pl
from jax.experimental.pallas import tpu as pltpu
from jax.sharding import PartitionSpec as P

MESH = pl.DeviceIdType.MESH
F32, BF16, I32 = jnp.float32, jnp.bfloat16, jnp.int32

learning_rate = 0.5
epsilon = 1e-08

GROUP = 64
CAP = 32
BLOCKS = 8
ROWS = 128
PART = 6
D = 128
LOOKUPS = 1024
FIRST, HOLDERS = 2, 4
EACH, PIECE = 4, 64
HELD = EACH * PIECE
PIECES = HOLDERS * EACH


def dot(a, b):
    return lax.dot_general(a, b, (((1,), (0,)), ((), ())), preferred_element_type=F32)


def dot_t(a, b):
    return lax.dot_general(a, b, (((1,), (1,)), ((), ())), preferred_element_type=F32)


def iota(shape, dim):
    return lax.broadcasted_iota(I32, shape, dim)


def halves(x):
    high = x.astype(BF16)
    return high, (x - high.astype(F32)).astype(BF16)


def rows_side_by_side(parts):
    return jnp.concatenate(parts, axis=1)


def gather_kernel(
    grad_hbm, len_hbm, slot_hbm, off_hbm, total_ref,
    grad_ref, len_ref, slot_ref, off_ref, sbuf, rbuf, rhl, looked, partial,
    left_in, left_side, right_in, right_side,
    copy_sem, send_sem, recv_sem, red_send,
    left_sem, left_side_sem, right_sem, right_side_sem, out_send, out_sem,
):
    loads = [
        pltpu.make_async_copy(src, dst, copy_sem.at[i])
        for i, (src, dst) in enumerate(
            ((grad_hbm, grad_ref), (len_hbm, len_ref), (slot_hbm, slot_ref), (off_hbm, off_ref))
        )
    ]
    for load in loads:
        load.start()

    replica, shard = lax.axis_index("replica"), lax.axis_index("shard")
    high_z, within = lax.div(shard, 32), lax.rem(shard, 32)
    z = high_z * 16 + replica
    parity = lax.rem(z, 2)
    sign = 1 - 2 * parity

    def device(z_at, place):
        return (lax.rem(z_at, 16), lax.div(z_at, 16) * 32 + place)

    def number(plane, y_at, rest):
        return plane * 32 + lax.rem(y_at - lax.div(rest, 2) + 4, 4) * 8 + rest

    my_rest = lax.rem(within, 8)
    me = number(parity, lax.div(within, 8), my_rest)
    my_oct = lax.div(me, 8)

    def member(oct_at, rest):
        y_at = lax.rem(oct_at + lax.div(rest, 2), 4)
        return (
            replica - parity + lax.div(oct_at, 4),
            high_z * 32 + y_at * 8 + rest,
        )

    seat = parity * lax.div(31 - z, 2) + (1 - parity) * lax.div(z, 2)

    def along(steps):
        return device(lax.rem(z + sign * steps + 32, 32), within)

    left, right, far_left, far_right = along(-2), along(2), along(-4), along(4)
    twin, inner, twin_right, inner_left = along(1), along(-1), along(3), along(-3)

    barrier = pltpu.get_barrier_semaphore()

    def greet(i, carry):
        oct_at = lax.rem(my_oct + i, 8)
        plane = replica - parity + lax.div(oct_at, 4)
        for x_at in range(4):
            place = high_z * 32 + lax.rem(oct_at + x_at, 4) * 8 + x_at * 2
            for core in range(2):

                @pl.when(oct_at * 8 + x_at * 2 + core != me)
                def _():
                    pl.semaphore_signal(
                        barrier, inc=1, device_id=(plane, place + core), device_id_type=MESH
                    )

        return carry

    for other in (left, right, far_left, far_right, inner, twin_right, inner_left):
        pl.semaphore_signal(barrier, inc=1, device_id=other, device_id_type=MESH)
    lax.fori_loop(0, 8, greet, 0)
    for load in loads:
        load.wait()

    row, col = iota((128, 128), 0), iota((128, 128), 1)
    upto = (row <= col).astype(F32).astype(BF16)
    before = (row < col).astype(F32).astype(BF16)
    lengths = len_ref[...].astype(F32)
    ends = dot(jnp.broadcast_to(lengths, (8, 128)).astype(BF16), upto)[0:1, :]
    starts = ends - lengths
    position = iota((LOOKUPS, 128), 0).astype(F32)
    sample_hot = jnp.where((position >= starts) & (position < ends), 1.0, 0.0).astype(BF16)
    high, low = halves(grad_ref[...])
    looked[...] = dot(sample_hot, jnp.concatenate([high, low], axis=1)).astype(BF16)

    slots = slot_ref[...]
    listed = lax.rem(slots, BLOCKS)
    index = lax.div(slots, BLOCKS)
    owner = number(lax.div(index, 32), lax.rem(lax.div(index, 8), 4), lax.rem(index, 8))
    owner_hot = [
        jnp.where(owner[b : b + 1, :] == iota((GROUP, 128), 0), 1.0, 0.0) for b in range(8)
    ]
    counts = dot(jnp.concatenate(owner_hot, axis=0).astype(BF16), before)
    seen = jnp.zeros((GROUP, 1), F32)
    ranks = []
    for b in range(8):
        earlier = counts[b * GROUP : (b + 1) * GROUP, :] + seen
        ranks.append(jnp.sum(owner_hot[b] * earlier, axis=0, keepdims=True))
        seen = seen + jnp.sum(owner_hot[b], axis=1, keepdims=True)
    rank = rows_side_by_side(ranks)
    owner_row = rows_side_by_side([owner[b : b + 1, :] for b in range(8)])
    place = owner_row * CAP + rank.astype(I32)
    owners = rows_side_by_side([h.astype(BF16) for h in owner_hot])
    lane = rank.astype(I32) + CAP * lax.rem(me, 4)
    at_lane = lane == iota((128, LOOKUPS), 0)
    listed_row = rows_side_by_side([listed[b : b + 1, :] for b in range(8)]).astype(F32)
    offset_row = rows_side_by_side([off_ref[b : b + 1, :] for b in range(8)]).astype(F32)
    ids = 128.0 * dot_t(owners, jnp.where(at_lane, listed_row + 1.0, 0.0).astype(BF16)) + dot_t(
        owners, jnp.where(at_lane, offset_row, 0.0).astype(BF16)
    )
    for o in range(GROUP):
        sbuf[o, CAP : CAP + 1, :] = ids[o : o + 1, :]

    pl.semaphore_wait(barrier, GROUP + 6)

    def value_copy(o, src, target):
        return pltpu.make_async_remote_copy(
            sbuf.at[o, pl.ds(0, CAP + 1)], rbuf.at[src, pl.ds(0, CAP + 1)],
            send_sem.at[o], recv_sem.at[src],
            device_id=target, device_id_type=MESH,
        )

    def send(i, carry):
        oct_at = lax.rem(my_oct + 1 + i, 8)
        hot = jnp.where(place - oct_at * 256 == iota((256, LOOKUPS), 0), 1.0, 0.0).astype(BF16)
        both = dot(hot, looked[...])
        sbuf[pl.ds(oct_at * 8, 8), pl.ds(0, CAP), :] = (both[:, :D] + both[:, D:]).reshape(8, CAP, D)
        for r in range(8):
            rest = lax.rem(my_rest + r, 8)
            o = oct_at * 8 + rest

            @pl.when(o != me)
            def _():
                value_copy(o, me, member(oct_at, rest)).start()

        return carry

    lax.fori_loop(0, 8, send, 0)
    rbuf[me, pl.ds(0, CAP), :] = sbuf[me, pl.ds(0, CAP), :]
    rbuf[me, pl.ds(CAP, 1), :] = sbuf[me, pl.ds(CAP, 1), :]

    def split_rows(src):
        high, low = halves(rbuf[src, pl.ds(0, CAP), :])
        rows = pl.ds(pl.multiple_of(src * CAP, CAP), CAP)
        rhl[rows, pl.ds(0, D)] = high
        rhl[rows, pl.ds(D, D)] = low

    split_rows(me)

    def arrive(i, carry):
        src = lax.rem(me + GROUP - i, GROUP)
        value_copy(src, src, left).wait_recv()
        split_rows(src)
        return carry

    lax.fori_loop(1, GROUP, arrive, 0)

    id_row = rows_side_by_side(
        [sum(rbuf[4 * g + r, CAP : CAP + 1, :] for r in range(4)) for g in range(16)]
    ).astype(I32)

    def own_pieces(h):
        hot = jnp.where(
            id_row - (h * HELD + ROWS) == iota((HELD, GROUP * CAP), 0), 1.0, 0.0
        ).astype(BF16)
        both = dot(hot, rhl[...])
        partial[pl.ds(h * EACH, EACH)] = (both[:, :D] + both[:, D:]).reshape(EACH, PIECE, D)

    def hop(q, into, sem, target):
        return pltpu.make_async_remote_copy(
            partial.at[q], into.at[q], red_send.at[q], sem.at[q],
            device_id=target, device_id_type=MESH,
        )

    def side_step(h, into, sem, target):
        @pl.when(h < HOLDERS)
        def _():
            own_pieces(h)

            def one(k, carry):
                hop(h * EACH + k, into, sem, target).start()
                return carry

            lax.fori_loop(0, EACH, one, 0)

    def place_of(steps):
        return lax.rem(seat - FIRST + steps + 32, 16)

    def reduce_step(t, carry):
        ahead = 8 - 2 * t
        h_left, h_right = place_of(-ahead), place_of(ahead)
        leads_left, leads_right = h_left < HOLDERS, (h_right < HOLDERS) & (t > 0)

        @pl.when(leads_left & (t == 0))
        def _():
            own_pieces(h_left)

            def one(k, carry):
                hop(h_left * EACH + k, left_in, left_sem, far_left).start()
                return carry

            lax.fori_loop(0, EACH, one, 0)

        side_step(place_of(1 - ahead), left_side, left_side_sem, left)
        side_step(place_of(ahead - 1), right_side, right_side_sem, right)

        @pl.when(leads_left & (t > 0))
        def _():
            own_pieces(h_left)

        @pl.when(leads_right)
        def _():
            own_pieces(h_right)

        def one(k, carry):
            @pl.when(leads_left & (t > 0))
            def _():
                q = h_left * EACH + k
                hop(q, left_side, left_side_sem, left).wait_recv()
                hop(q, left_in, left_sem, far_left).wait_recv()
                partial[q] = partial[q] + left_side[q] + left_in[q]
                hop(q, left_in, left_sem, far_left).start()

            @pl.when(leads_right)
            def _():
                q = h_right * EACH + k
                hop(q, right_side, right_side_sem, right).wait_recv()

                @pl.when(t > 1)
                def _():
                    hop(q, right_in, right_sem, far_right).wait_recv()
                    partial[q] = partial[q] + right_in[q]

                partial[q] = partial[q] + right_side[q]
                hop(q, right_in, right_sem, far_right).start()

            return carry

        lax.fori_loop(0, EACH, one, 0)
        return carry

    def gone(i, carry):
        value_copy(lax.rem(me + i, GROUP), me, left).wait_send()
        return carry

    reduce_step(0, 0)
    lax.fori_loop(1, GROUP, gone, 0)
    lax.fori_loop(1, 4, reduce_step, 0)

    def out_copy(q, way, target):
        return pltpu.make_async_remote_copy(
            total_ref.at[q], total_ref.at[q], out_send.at[q, way], out_sem.at[q],
            device_id=target, device_id_type=MESH,
        )

    main = seat < 8
    mine = seat - FIRST
    holds = (mine >= 0) & (mine < HOLDERS)

    @pl.when(holds)
    def _():
        own_pieces(mine)

        def one(k, carry):
            q = mine * EACH + k
            hop(q, left_side, left_side_sem, left).wait_recv()
            hop(q, right_side, right_side_sem, right).wait_recv()
            hop(q, right_in, right_sem, far_right).wait_recv()
            hop(q, left_in, left_sem, far_left).wait_recv()
            total_ref[q] = (
                partial[q] + left_side[q] + right_side[q] + left_in[q] + right_in[q]
            )
            out_copy(q, 0, far_left).start()
            out_copy(q, 1, far_right).start()
            return carry

        lax.fori_loop(0, EACH, one, 0)

    def reduced(q, carry):
        @pl.when(lax.div(q, EACH) != mine)
        def _():
            hop(q, left_in, left_sem, left).wait_send()

        return carry

    lax.fori_loop(0, PIECES, reduced, 0)

    @pl.when(main)
    def _():
        def pass_on(i, carry):
            away = i + 2 - 2 * lax.rem(i, 2)
            even = lax.rem(away, 2) == 0

            def one(k, carry):
                @pl.when((mine + away >= 0) & (mine + away < HOLDERS))
                def _():
                    q = (mine + away) * EACH + k
                    out_copy(q, 0, left).wait_recv()

                    @pl.when(even & (seat >= 2))
                    def _():
                        out_copy(q, 0, far_left).start()

                    @pl.when(even & (seat == 1))
                    def _():
                        out_copy(q, 0, left).start()

                    @pl.when(even)
                    def _():
                        out_copy(q, 1, right).start()

                    @pl.when((away != 5) & ((away != 3) | (seat == 0)))
                    def _():
                        out_copy(q, 2, twin).start()

                    @pl.when(away == 4)
                    def _():
                        out_copy(q, 3, twin_right).start()

                    @pl.when((away == 4) & (seat == 1))
                    def _():
                        out_copy(q, 4, inner).start()

                @pl.when((mine - away >= 0) & (mine - away < HOLDERS))
                def _():
                    q = (mine - away) * EACH + k
                    out_copy(q, 1, right).wait_recv()

                    @pl.when(even & (seat <= 5))
                    def _():
                        out_copy(q, 0, far_right).start()

                    @pl.when(even & (seat == 6))
                    def _():
                        out_copy(q, 0, right).start()

                    @pl.when(even)
                    def _():
                        out_copy(q, 1, left).start()

                    @pl.when((away != 5) & ((away != 3) | (seat == 7)))
                    def _():
                        out_copy(q, 2, inner).start()

                    @pl.when(away == 4)
                    def _():
                        out_copy(q, 3, inner_left).start()

                    @pl.when(((away != 5) & (seat == 7)) | ((away == 4) & (seat == 6)))
                    def _():
                        out_copy(q, 4, twin).start()

                    @pl.when((away == 4) & (seat == 6))
                    def _():
                        out_copy(q, 5, twin_right).start()

                return carry

            return lax.fori_loop(0, EACH, one, carry)

        lax.fori_loop(0, 6, pass_on, 0)

        def sent(q, carry):
            h = lax.div(q, EACH)
            even = lax.rem(h + FIRST + seat, 2) == 0
            outer = ((h > mine) & (seat > 0)) | ((h < mine) & (seat < 7)) | (h == mine)

            @pl.when(even & outer)
            def _():
                out_copy(q, 0, left).wait_send()

            @pl.when(even)
            def _():
                out_copy(q, 1, right).wait_send()

            up = h - mine
            four = (up == 4) | (up == -4)
            five = (up == 5) | (up == -5)
            three = ((up == 3) & (seat > 0)) | ((up == -3) & (seat < 7))

            @pl.when((up != 0) & jnp.logical_not(five) & jnp.logical_not(three))
            def _():
                out_copy(q, 2, twin).wait_send()

            @pl.when(four)
            def _():
                out_copy(q, 3, twin).wait_send()

            @pl.when(
                ((up == 4) & (seat == 1))
                | ((up == -4) & (seat == 6))
                | ((seat == 7) & jnp.logical_not(five))
            )
            def _():
                out_copy(q, 4, twin).wait_send()

            @pl.when((up == -4) & (seat == 6))
            def _():
                out_copy(q, 5, twin).wait_send()

            return carry

        lax.fori_loop(0, PIECES, sent, 0)

    @pl.when(jnp.logical_not(main))
    def _():
        def land(q, carry):
            out_copy(q, 2, twin).wait_recv()
            return carry

        lax.fori_loop(0, PIECES, land, 0)


def update_kernel(
    touched_hbm, total_hbm, table_hbm, accum_hbm, table_out, accum_out,
    total_ref, table_ref, accum_ref, at_block, touched_ref, sem,
):
    load_total = pltpu.make_async_copy(total_hbm, total_ref, sem.at[0])
    load_total.start()
    load_touched = pltpu.make_async_copy(touched_hbm, touched_ref, sem.at[2])
    load_touched.start()
    def part(ref, c):
        return ref.at[pl.ds(c * PART * ROWS, PART * ROWS)]

    parts = table_ref.shape[0] // (PART * ROWS)
    load_table = [
        pltpu.make_async_copy(part(table_hbm, c), part(table_ref, c), sem.at[5 + c])
        for c in range(parts)
    ]
    save_table = [
        pltpu.make_async_copy(part(table_ref, c), part(table_out, c), sem.at[5 + parts + c])
        for c in range(parts)
    ]
    load_accum = pltpu.make_async_copy(accum_hbm, accum_ref, sem.at[1])
    load_accum.start()
    for load in load_table:
        load.start()
    load_total.wait()
    squares = [
        jnp.sum(total_ref[j] * total_ref[j], axis=1, keepdims=True) * (1.0 / D)
        for j in range(BLOCKS)
    ]
    load_touched.wait()
    load_accum.wait()
    at_block[...] = jnp.zeros_like(at_block)
    for j in range(BLOCKS):
        at_block[j : j + 1, :] = accum_ref[pl.ds(touched_ref[j], 1), :]
    old = at_block[...].T
    new = old
    lanes = iota((ROWS, ROWS), 1)
    steps = []
    for j in range(BLOCKS):
        rows = old[:, j : j + 1] + squares[j]
        new = jnp.where(lanes == j, rows, new)
        steps.append(learning_rate / (jnp.sqrt(rows) + epsilon))
    at_block[...] = new.T
    for j in range(BLOCKS):
        accum_ref[pl.ds(touched_ref[j], 1), :] = at_block[j : j + 1, :]
    save_accum = pltpu.make_async_copy(accum_ref, accum_out, sem.at[3])
    save_accum.start()
    for c in range(parts):
        load_table[c].wait()
        for j in range(BLOCKS):

            @pl.when(lax.div(touched_ref[j], PART) == c)
            def _():
                rows = pl.ds(pl.multiple_of(touched_ref[j] * ROWS, ROWS), ROWS)
                table_ref[rows, :] = table_ref[rows, :] - total_ref[j] * steps[j]

        save_table[c].start()
    save_accum.wait()
    for save in save_table:
        save.wait()


def on_device(
    pooled_grad, bag_lengths, slot_ids, offsets, touched_blocks, embedding_table, accumulator
):
    vmem = pl.BlockSpec(memory_space=pltpu.VMEM)
    hbm = pl.BlockSpec(memory_space=pltpu.HBM)
    dma = pltpu.SemaphoreType.DMA
    pieces = pltpu.VMEM((PIECES, PIECE, D), F32)
    total = pl.pallas_call(
        gather_kernel,
        out_shape=jax.ShapeDtypeStruct((PIECES, PIECE, D), F32),
        in_specs=[hbm] * 4,
        out_specs=vmem,
        scratch_shapes=[
            pltpu.VMEM((128, D), F32),
            pltpu.VMEM((1, 128), I32),
            pltpu.VMEM((8, 128), I32),
            pltpu.VMEM((8, 128), I32),
            pltpu.VMEM((GROUP, CAP + 8, D), F32),
            pltpu.VMEM((GROUP, CAP + 8, D), F32),
            pltpu.VMEM((GROUP * CAP, 2 * D), BF16),
            pltpu.VMEM((LOOKUPS, 2 * D), BF16),
            pieces, pieces, pieces, pieces, pieces,
            dma((4,)),
            dma((GROUP,)), dma((GROUP,)),
            dma((PIECES,)), dma((PIECES,)), dma((PIECES,)), dma((PIECES,)), dma((PIECES,)),
            dma((PIECES, 6)), dma((PIECES,)),
        ],
        compiler_params=pltpu.CompilerParams(
            collective_id=0, has_side_effects=True, vmem_limit_bytes=63 << 20
        ),
        name="exchange",
    )(pooled_grad, bag_lengths, slot_ids.reshape(8, 128), offsets.reshape(8, 128))
    rows = embedding_table.shape[0]
    new_table, new_accumulator = pl.pallas_call(
        update_kernel,
        out_shape=(
            jax.ShapeDtypeStruct((rows, D), F32),
            jax.ShapeDtypeStruct((rows // ROWS, ROWS), F32),
        ),
        in_specs=[hbm, hbm, hbm, hbm],
        out_specs=(hbm, hbm),
        scratch_shapes=[
            pltpu.VMEM((BLOCKS, ROWS, D), F32),
            pltpu.VMEM((rows, D), F32),
            pltpu.VMEM((rows // ROWS, ROWS), F32),
            pltpu.VMEM((ROWS, ROWS), F32),
            pltpu.SMEM((BLOCKS,), I32),
            dma((5 + 2 * (rows // (PART * ROWS)),)),
        ],
        compiler_params=pltpu.CompilerParams(vmem_limit_bytes=63 << 20),
        name="adagrad",
    )(
        touched_blocks, total.reshape(BLOCKS, ROWS, D), embedding_table,
        accumulator.reshape(rows // ROWS, ROWS),
    )
    return new_table, new_accumulator.reshape(rows)


def solution(mesh):
    return jax.shard_map(
        on_device,
        mesh=mesh,
        in_specs=(
            P(("replica", "shard"), None),
            P(("replica", "shard"), None),
            P(("replica", "shard")),
            P(("replica", "shard")),
            P("shard"),
            P("shard", None),
            P("shard"),
        ),
        out_specs=(P("shard", None), P("shard")),
        check_vma=False,
    )
```

```python
import jax
import jax.numpy as jnp
from jax import lax
from jax.experimental import pallas as pl
from jax.experimental.pallas import tpu as pltpu
from jax.sharding import PartitionSpec as P

MESH = pl.DeviceIdType.MESH
F32, BF16, I32 = jnp.float32, jnp.bfloat16, jnp.int32

learning_rate = 0.5
epsilon = 1e-08

GROUP = 64
CAP = 32
BLOCKS = 8
ROWS = 128
PART = 6
D = 128
LOOKUPS = 1024
FIRST, HOLDERS = 2, 4
EACH, PIECE = 4, 64
HELD = EACH * PIECE
PIECES = HOLDERS * EACH


def dot(a, b):
    return lax.dot_general(a, b, (((1,), (0,)), ((), ())), preferred_element_type=F32)


def dot_t(a, b):
    return lax.dot_general(a, b, (((1,), (1,)), ((), ())), preferred_element_type=F32)


def iota(shape, dim):
    return lax.broadcasted_iota(I32, shape, dim)


def halves(x):
    high = x.astype(BF16)
    return high, (x - high.astype(F32)).astype(BF16)


def rows_side_by_side(parts):
    return jnp.concatenate(parts, axis=1)


def gather_kernel(
    grad_hbm, len_hbm, slot_hbm, off_hbm, total_hbm,
    total_ref, grad_ref, len_ref, slot_ref, off_ref, sbuf, rbuf, rhl, looked, partial,
    left_in, left_side, right_in, right_side,
    copy_sem, send_sem, recv_sem, red_send,
    left_sem, left_side_sem, right_sem, right_side_sem, out_send, out_sem, save_sem,
):
    loads = [
        pltpu.make_async_copy(src, dst, copy_sem.at[i])
        for i, (src, dst) in enumerate(
            ((grad_hbm, grad_ref), (len_hbm, len_ref), (slot_hbm, slot_ref), (off_hbm, off_ref))
        )
    ]
    for load in loads:
        load.start()

    replica, shard = lax.axis_index("replica"), lax.axis_index("shard")
    high_z, within = lax.div(shard, 32), lax.rem(shard, 32)
    z = high_z * 16 + replica
    parity = lax.rem(z, 2)
    sign = 1 - 2 * parity

    def device(z_at, place):
        return (lax.rem(z_at, 16), lax.div(z_at, 16) * 32 + place)

    def number(plane, y_at, rest):
        return plane * 32 + lax.rem(y_at - lax.div(rest, 2) + 4, 4) * 8 + rest

    my_rest = lax.rem(within, 8)
    me = number(parity, lax.div(within, 8), my_rest)
    my_oct = lax.div(me, 8)

    def member(oct_at, rest):
        y_at = lax.rem(oct_at + lax.div(rest, 2), 4)
        return (
            replica - parity + lax.div(oct_at, 4),
            high_z * 32 + y_at * 8 + rest,
        )

    seat = parity * lax.div(31 - z, 2) + (1 - parity) * lax.div(z, 2)

    def along(steps):
        return device(lax.rem(z + sign * steps + 32, 32), within)

    left, right, far_left, far_right = along(-2), along(2), along(-4), along(4)
    twin, inner, twin_right, inner_left = along(1), along(-1), along(3), along(-3)

    barrier = pltpu.get_barrier_semaphore()

    def greet(i, carry):
        oct_at = lax.rem(my_oct + i, 8)
        plane = replica - parity + lax.div(oct_at, 4)
        for x_at in range(4):
            place = high_z * 32 + lax.rem(oct_at + x_at, 4) * 8 + x_at * 2
            for core in range(2):

                @pl.when(oct_at * 8 + x_at * 2 + core != me)
                def _():
                    pl.semaphore_signal(
                        barrier, inc=1, device_id=(plane, place + core), device_id_type=MESH
                    )

        return carry

    for other in (left, right, far_left, far_right, inner, twin_right, inner_left):
        pl.semaphore_signal(barrier, inc=1, device_id=other, device_id_type=MESH)
    lax.fori_loop(0, 8, greet, 0)
    for load in loads:
        load.wait()

    row, col = iota((128, 128), 0), iota((128, 128), 1)
    upto = (row <= col).astype(F32).astype(BF16)
    before = (row < col).astype(F32).astype(BF16)
    lengths = len_ref[...].astype(F32)
    ends = dot(jnp.broadcast_to(lengths, (8, 128)).astype(BF16), upto)[0:1, :]
    starts = ends - lengths
    position = iota((LOOKUPS, 128), 0).astype(F32)
    sample_hot = jnp.where((position >= starts) & (position < ends), 1.0, 0.0).astype(BF16)
    high, low = halves(grad_ref[...])
    looked[...] = dot(sample_hot, jnp.concatenate([high, low], axis=1)).astype(BF16)

    slots = slot_ref[...]
    listed = lax.rem(slots, BLOCKS)
    index = lax.div(slots, BLOCKS)
    owner = number(lax.div(index, 32), lax.rem(lax.div(index, 8), 4), lax.rem(index, 8))
    owner_hot = [
        jnp.where(owner[b : b + 1, :] == iota((GROUP, 128), 0), 1.0, 0.0) for b in range(8)
    ]
    counts = dot(jnp.concatenate(owner_hot, axis=0).astype(BF16), before)
    seen = jnp.zeros((GROUP, 1), F32)
    ranks = []
    for b in range(8):
        earlier = counts[b * GROUP : (b + 1) * GROUP, :] + seen
        ranks.append(jnp.sum(owner_hot[b] * earlier, axis=0, keepdims=True))
        seen = seen + jnp.sum(owner_hot[b], axis=1, keepdims=True)
    rank = rows_side_by_side(ranks)
    owner_row = rows_side_by_side([owner[b : b + 1, :] for b in range(8)])
    place = owner_row * CAP + rank.astype(I32)
    owners = rows_side_by_side([h.astype(BF16) for h in owner_hot])
    lane = rank.astype(I32) + CAP * lax.rem(me, 4)
    at_lane = lane == iota((128, LOOKUPS), 0)
    listed_row = rows_side_by_side([listed[b : b + 1, :] for b in range(8)]).astype(F32)
    offset_row = rows_side_by_side([off_ref[b : b + 1, :] for b in range(8)]).astype(F32)
    ids = 128.0 * dot_t(owners, jnp.where(at_lane, listed_row + 1.0, 0.0).astype(BF16)) + dot_t(
        owners, jnp.where(at_lane, offset_row, 0.0).astype(BF16)
    )
    for o in range(GROUP):
        sbuf[o, CAP : CAP + 1, :] = ids[o : o + 1, :]

    pl.semaphore_wait(barrier, GROUP + 6)

    def value_copy(o, src, target):
        return pltpu.make_async_remote_copy(
            sbuf.at[o, pl.ds(0, CAP + 1)], rbuf.at[src, pl.ds(0, CAP + 1)],
            send_sem.at[o], recv_sem.at[src],
            device_id=target, device_id_type=MESH,
        )

    def send(i, carry):
        oct_at = lax.rem(my_oct + 1 + i, 8)
        hot = jnp.where(place - oct_at * 256 == iota((256, LOOKUPS), 0), 1.0, 0.0).astype(BF16)
        both = dot(hot, looked[...])
        sbuf[pl.ds(oct_at * 8, 8), pl.ds(0, CAP), :] = (both[:, :D] + both[:, D:]).reshape(8, CAP, D)
        for r in range(8):
            rest = lax.rem(my_rest + r, 8)
            o = oct_at * 8 + rest

            @pl.when(o != me)
            def _():
                value_copy(o, me, member(oct_at, rest)).start()

        return carry

    lax.fori_loop(0, 8, send, 0)
    rbuf[me, pl.ds(0, CAP), :] = sbuf[me, pl.ds(0, CAP), :]
    rbuf[me, pl.ds(CAP, 1), :] = sbuf[me, pl.ds(CAP, 1), :]

    def split_rows(src):
        high, low = halves(rbuf[src, pl.ds(0, CAP), :])
        rows = pl.ds(pl.multiple_of(src * CAP, CAP), CAP)
        rhl[rows, pl.ds(0, D)] = high
        rhl[rows, pl.ds(D, D)] = low

    split_rows(me)

    def arrive(i, carry):
        src = lax.rem(me + GROUP - i, GROUP)
        value_copy(src, src, left).wait_recv()
        split_rows(src)
        return carry

    lax.fori_loop(1, GROUP, arrive, 0)

    id_row = rows_side_by_side(
        [sum(rbuf[4 * g + r, CAP : CAP + 1, :] for r in range(4)) for g in range(16)]
    ).astype(I32)

    def own_pieces(h):
        hot = jnp.where(
            id_row - (h * HELD + ROWS) == iota((HELD, GROUP * CAP), 0), 1.0, 0.0
        ).astype(BF16)
        both = dot(hot, rhl[...])
        partial[pl.ds(h * EACH, EACH)] = (both[:, :D] + both[:, D:]).reshape(EACH, PIECE, D)

    def hop(q, into, sem, target):
        return pltpu.make_async_remote_copy(
            partial.at[q], into.at[q], red_send.at[q], sem.at[q],
            device_id=target, device_id_type=MESH,
        )

    def side_step(h, into, sem, target):
        @pl.when(h < HOLDERS)
        def _():
            own_pieces(h)

            def one(k, carry):
                hop(h * EACH + k, into, sem, target).start()
                return carry

            lax.fori_loop(0, EACH, one, 0)

    def place_of(steps):
        return lax.rem(seat - FIRST + steps + 32, 16)

    def reduce_step(t, carry):
        ahead = 8 - 2 * t
        h_left, h_right = place_of(-ahead), place_of(ahead)
        leads_left, leads_right = h_left < HOLDERS, (h_right < HOLDERS) & (t > 0)

        @pl.when(leads_left & (t == 0))
        def _():
            own_pieces(h_left)

            def one(k, carry):
                hop(h_left * EACH + k, left_in, left_sem, far_left).start()
                return carry

            lax.fori_loop(0, EACH, one, 0)

        side_step(place_of(1 - ahead), left_side, left_side_sem, left)
        side_step(place_of(ahead - 1), right_side, right_side_sem, right)

        @pl.when(leads_left & (t > 0))
        def _():
            own_pieces(h_left)

        @pl.when(leads_right)
        def _():
            own_pieces(h_right)

        def one(k, carry):
            @pl.when(leads_left & (t > 0))
            def _():
                q = h_left * EACH + k
                hop(q, left_side, left_side_sem, left).wait_recv()
                hop(q, left_in, left_sem, far_left).wait_recv()
                partial[q] = partial[q] + left_side[q] + left_in[q]
                hop(q, left_in, left_sem, far_left).start()

            @pl.when(leads_right)
            def _():
                q = h_right * EACH + k
                hop(q, right_side, right_side_sem, right).wait_recv()

                @pl.when(t > 1)
                def _():
                    hop(q, right_in, right_sem, far_right).wait_recv()
                    partial[q] = partial[q] + right_in[q]

                partial[q] = partial[q] + right_side[q]
                hop(q, right_in, right_sem, far_right).start()

            return carry

        lax.fori_loop(0, EACH, one, 0)
        return carry

    def gone(i, carry):
        value_copy(lax.rem(me + i, GROUP), me, left).wait_send()
        return carry

    reduce_step(0, 0)
    lax.fori_loop(1, GROUP, gone, 0)
    lax.fori_loop(1, 4, reduce_step, 0)

    def out_copy(q, way, target):
        return pltpu.make_async_remote_copy(
            total_ref.at[q], total_ref.at[q], out_send.at[q, way], out_sem.at[q],
            device_id=target, device_id_type=MESH,
        )

    def save(q):
        return pltpu.make_async_copy(total_ref.at[q], total_hbm.at[q], save_sem.at[q])

    main = seat < 8
    mine = seat - FIRST
    holds = (mine >= 0) & (mine < HOLDERS)

    @pl.when(holds)
    def _():
        own_pieces(mine)

        def one(k, carry):
            q = mine * EACH + k
            hop(q, left_side, left_side_sem, left).wait_recv()
            hop(q, right_side, right_side_sem, right).wait_recv()
            hop(q, right_in, right_sem, far_right).wait_recv()
            hop(q, left_in, left_sem, far_left).wait_recv()
            total_ref[q] = (
                partial[q] + left_side[q] + right_side[q] + left_in[q] + right_in[q]
            )
            out_copy(q, 0, far_left).start()
            out_copy(q, 1, far_right).start()
            save(q).start()
            return carry

        lax.fori_loop(0, EACH, one, 0)

    def reduced(q, carry):
        @pl.when(lax.div(q, EACH) != mine)
        def _():
            hop(q, left_in, left_sem, left).wait_send()

        return carry

    lax.fori_loop(0, PIECES, reduced, 0)

    @pl.when(main)
    def _():
        def pass_on(i, carry):
            away = i + 2 - 2 * lax.rem(i, 2)
            even = lax.rem(away, 2) == 0

            def one(k, carry):
                @pl.when((mine + away >= 0) & (mine + away < HOLDERS))
                def _():
                    q = (mine + away) * EACH + k
                    out_copy(q, 0, left).wait_recv()

                    @pl.when(even & (seat >= 2))
                    def _():
                        out_copy(q, 0, far_left).start()

                    @pl.when(even & (seat == 1))
                    def _():
                        out_copy(q, 0, left).start()

                    @pl.when(even)
                    def _():
                        out_copy(q, 1, right).start()

                    @pl.when((away != 5) & ((away != 3) | (seat == 0)))
                    def _():
                        out_copy(q, 2, twin).start()

                    @pl.when(away == 4)
                    def _():
                        out_copy(q, 3, twin_right).start()

                    @pl.when((away == 4) & (seat == 1))
                    def _():
                        out_copy(q, 4, inner).start()

                    save(q).start()

                @pl.when((mine - away >= 0) & (mine - away < HOLDERS))
                def _():
                    q = (mine - away) * EACH + k
                    out_copy(q, 1, right).wait_recv()

                    @pl.when(even & (seat <= 5))
                    def _():
                        out_copy(q, 0, far_right).start()

                    @pl.when(even & (seat == 6))
                    def _():
                        out_copy(q, 0, right).start()

                    @pl.when(even)
                    def _():
                        out_copy(q, 1, left).start()

                    @pl.when((away != 5) & ((away != 3) | (seat == 7)))
                    def _():
                        out_copy(q, 2, inner).start()

                    @pl.when(away == 4)
                    def _():
                        out_copy(q, 3, inner_left).start()

                    @pl.when(((away != 5) & (seat == 7)) | ((away == 4) & (seat == 6)))
                    def _():
                        out_copy(q, 4, twin).start()

                    @pl.when((away == 4) & (seat == 6))
                    def _():
                        out_copy(q, 5, twin_right).start()

                    save(q).start()

                return carry

            return lax.fori_loop(0, EACH, one, carry)

        lax.fori_loop(0, 6, pass_on, 0)

        def sent(q, carry):
            h = lax.div(q, EACH)
            even = lax.rem(h + FIRST + seat, 2) == 0
            outer = ((h > mine) & (seat > 0)) | ((h < mine) & (seat < 7)) | (h == mine)

            @pl.when(even & outer)
            def _():
                out_copy(q, 0, left).wait_send()

            @pl.when(even)
            def _():
                out_copy(q, 1, right).wait_send()

            up = h - mine
            four = (up == 4) | (up == -4)
            five = (up == 5) | (up == -5)
            three = ((up == 3) & (seat > 0)) | ((up == -3) & (seat < 7))

            @pl.when((up != 0) & jnp.logical_not(five) & jnp.logical_not(three))
            def _():
                out_copy(q, 2, twin).wait_send()

            @pl.when(four)
            def _():
                out_copy(q, 3, twin).wait_send()

            @pl.when(
                ((up == 4) & (seat == 1))
                | ((up == -4) & (seat == 6))
                | ((seat == 7) & jnp.logical_not(five))
            )
            def _():
                out_copy(q, 4, twin).wait_send()

            @pl.when((up == -4) & (seat == 6))
            def _():
                out_copy(q, 5, twin).wait_send()

            return carry

        lax.fori_loop(0, PIECES, sent, 0)

    @pl.when(jnp.logical_not(main))
    def _():
        def land(q, carry):
            out_copy(q, 2, twin).wait_recv()
            save(q).start()
            return carry

        lax.fori_loop(0, PIECES, land, 0)

    def saved(q, carry):
        save(q).wait()
        return carry

    lax.fori_loop(0, PIECES, saved, 0)


def update_kernel(
    touched_hbm, total_hbm, table_hbm, accum_hbm, table_out, accum_out,
    total_ref, table_ref, accum_ref, at_block, touched_ref, sem,
):
    load_total = pltpu.make_async_copy(total_hbm, total_ref, sem.at[0])
    load_total.start()
    load_touched = pltpu.make_async_copy(touched_hbm, touched_ref, sem.at[2])
    load_touched.start()
    def part(ref, c):
        return ref.at[pl.ds(c * PART * ROWS, PART * ROWS)]

    parts = table_ref.shape[0] // (PART * ROWS)
    load_table = [
        pltpu.make_async_copy(part(table_hbm, c), part(table_ref, c), sem.at[5 + c])
        for c in range(parts)
    ]
    save_table = [
        pltpu.make_async_copy(part(table_ref, c), part(table_out, c), sem.at[5 + parts + c])
        for c in range(parts)
    ]
    load_accum = pltpu.make_async_copy(accum_hbm, accum_ref, sem.at[1])
    load_accum.start()
    for load in load_table:
        load.start()
    load_total.wait()
    squares = [
        jnp.sum(total_ref[j] * total_ref[j], axis=1, keepdims=True) * (1.0 / D)
        for j in range(BLOCKS)
    ]
    load_touched.wait()
    load_accum.wait()
    at_block[...] = jnp.zeros_like(at_block)
    for j in range(BLOCKS):
        at_block[j : j + 1, :] = accum_ref[pl.ds(touched_ref[j], 1), :]
    old = at_block[...].T
    new = old
    lanes = iota((ROWS, ROWS), 1)
    steps = []
    for j in range(BLOCKS):
        rows = old[:, j : j + 1] + squares[j]
        new = jnp.where(lanes == j, rows, new)
        steps.append(learning_rate / (jnp.sqrt(rows) + epsilon))
    at_block[...] = new.T
    for j in range(BLOCKS):
        accum_ref[pl.ds(touched_ref[j], 1), :] = at_block[j : j + 1, :]
    save_accum = pltpu.make_async_copy(accum_ref, accum_out, sem.at[3])
    save_accum.start()
    for c in range(parts):
        load_table[c].wait()
        for j in range(BLOCKS):

            @pl.when(lax.div(touched_ref[j], PART) == c)
            def _():
                rows = pl.ds(pl.multiple_of(touched_ref[j] * ROWS, ROWS), ROWS)
                table_ref[rows, :] = table_ref[rows, :] - total_ref[j] * steps[j]

        save_table[c].start()
    save_accum.wait()
    for save in save_table:
        save.wait()


def on_device(
    pooled_grad, bag_lengths, slot_ids, offsets, touched_blocks, embedding_table, accumulator
):
    hbm = pl.BlockSpec(memory_space=pltpu.HBM)
    dma = pltpu.SemaphoreType.DMA
    pieces = pltpu.VMEM((PIECES, PIECE, D), F32)
    total = pl.pallas_call(
        gather_kernel,
        out_shape=jax.ShapeDtypeStruct((PIECES, PIECE, D), F32),
        in_specs=[hbm] * 4,
        out_specs=hbm,
        scratch_shapes=[
            pieces,
            pltpu.VMEM((128, D), F32),
            pltpu.VMEM((1, 128), I32),
            pltpu.VMEM((8, 128), I32),
            pltpu.VMEM((8, 128), I32),
            pltpu.VMEM((GROUP, CAP + 8, D), F32),
            pltpu.VMEM((GROUP, CAP + 8, D), F32),
            pltpu.VMEM((GROUP * CAP, 2 * D), BF16),
            pltpu.VMEM((LOOKUPS, 2 * D), BF16),
            pieces, pieces, pieces, pieces, pieces,
            dma((4,)),
            dma((GROUP,)), dma((GROUP,)),
            dma((PIECES,)), dma((PIECES,)), dma((PIECES,)), dma((PIECES,)), dma((PIECES,)),
            dma((PIECES, 6)), dma((PIECES,)), dma((PIECES,)),
        ],
        compiler_params=pltpu.CompilerParams(
            collective_id=0, has_side_effects=True, vmem_limit_bytes=63 << 20
        ),
        name="exchange",
    )(pooled_grad, bag_lengths, slot_ids.reshape(8, 128), offsets.reshape(8, 128))
    rows = embedding_table.shape[0]
    new_table, new_accumulator = pl.pallas_call(
        update_kernel,
        out_shape=(
            jax.ShapeDtypeStruct((rows, D), F32),
            jax.ShapeDtypeStruct((rows // ROWS, ROWS), F32),
        ),
        in_specs=[hbm, hbm, hbm, hbm],
        out_specs=(hbm, hbm),
        scratch_shapes=[
            pltpu.VMEM((BLOCKS, ROWS, D), F32),
            pltpu.VMEM((rows, D), F32),
            pltpu.VMEM((rows // ROWS, ROWS), F32),
            pltpu.VMEM((ROWS, ROWS), F32),
            pltpu.SMEM((BLOCKS,), I32),
            dma((5 + 2 * (rows // (PART * ROWS)),)),
        ],
        compiler_params=pltpu.CompilerParams(vmem_limit_bytes=63 << 20),
        name="adagrad",
    )(
        touched_blocks, total.reshape(BLOCKS, ROWS, D), embedding_table,
        accumulator.reshape(rows // ROWS, ROWS),
    )
    return new_table, new_accumulator.reshape(rows)


def solution(mesh):
    return jax.shard_map(
        on_device,
        mesh=mesh,
        in_specs=(
            P(("replica", "shard"), None),
            P(("replica", "shard"), None),
            P(("replica", "shard")),
            P(("replica", "shard")),
            P("shard"),
            P("shard", None),
            P("shard"),
        ),
        out_specs=(P("shard", None), P("shard")),
        check_vma=False,
    )
```
